32 devices in a mesh: tracer: 4 (over y, x), tile: 8 (over z, core).
Axes of the slice: x: 2, y: 2, z: 4, core: 2. Of those that a mesh axis runs over, the one named last changes fastest.
Arguments:
- tracers: float32 [192, 8, 128, 128], P('tracer', None, 'tile'), may hold values from 0.1 to 2
- air_mass: float32 [4, 8, 128, 128], P('tracer', None, 'tile'), may hold values from 1 to 2
- flux_x: float32 [4, 8, 128, 128], P('tracer', None, 'tile'), may hold values from -0.2 to 0.2
- flux_y: float32 [4, 8, 128, 128], P('tracer', None, 'tile'), may hold values from -0.2 to 0.2
- flux_z: float32 [4, 8, 128, 128], P('tracer', None, 'tile'), may hold values from -0.05 to 0.05
- reactants: int32 [512, 2], replicated, may hold values from 0 to 191
- products: int32 [512, 192], replicated, may hold values 0 or 1
- rate_coeff: float32 [512], replicated, may hold values from 0.01 to 0.1
- record_of_step: int32 [2], replicated, may hold values from 0 to 3
Outputs:
- tracers_out: float32 [192, 8, 128, 128], P('tracer', None, 'tile')
The draws below stay inside these ranges and needn't reach their ends.
Inputs may be any that keep to these rules, and one draw needn't show every extreme that they name: A reaction's two reactants may be the same tracer.
All inputs are finite; a program needn't handle non-finite values.
Results may differ from the reference program's by a relative error of at most 0.0014.
Values may be sent and summed in bfloat16 or wider, within the bound.
A program may use at most 128 MiB of HBM per device.

```python
import math
import jax
import jax.numpy as jnp
from jax import lax

TRACERS = 192
REACTIONS = 512
LEVELS = 8
STEPS = 2
NY = 128
NX = 128
N_TRACER = 4


def touch_ends(entries, stream_key, smallest, top_value):
    dims = entries.shape
    spot = [jax.random.randint(jax.random.fold_in(stream_key, axis), (), 0, dims[axis]) for axis in range(len(dims))]
    entries = entries.at[tuple(spot)].set(smallest)
    longest = dims.index(max(dims))
    spot[longest] = (spot[longest] + 1) % dims[longest]
    return entries.at[tuple(spot)].set(top_value)


def level_of(key, extent, split, low, high):
    def one(position, shards_of):
        steps = jax.random.uniform(jax.random.fold_in(jax.random.fold_in(key, 6), position), (shards_of,), jnp.float32, low / len(split), high / len(split))
        return jnp.repeat(jnp.exp(steps), extent[position] // shards_of).reshape((-1,) + (1,) * (len(extent) - position - 1))

    gain = one(*split[0])
    for cut in split[1:]:
        gain = gain * one(*cut)
    return gain


def setup_inputs(seed: int = 0) -> dict:
    streams_of = jax.random.split(jax.random.key(seed), 10)
    tracers = jnp.clip(jnp.exp(math.log(2.0) - 2.9957323 * jax.random.uniform(streams_of[0], (TRACERS, LEVELS, NX, NY), jnp.float32) ** level_of(streams_of[0], (TRACERS, LEVELS, NX, NY), ((0, 4), (2, 8)), -0.2, 0.2)), 0.1, 2.0)
    air_mass = jnp.clip(1.0 + 1.0 * jax.random.uniform(streams_of[1], (N_TRACER, LEVELS, NX, NY), jnp.float32) ** level_of(streams_of[1], (N_TRACER, LEVELS, NX, NY), ((0, 4), (2, 8)), -0.2, 0.2), 1.0, 2.0)
    flux_x = jnp.clip(jax.random.uniform(streams_of[2], (N_TRACER, LEVELS, NX, NY), jnp.float32, -0.2, 0.2) * level_of(streams_of[2], (N_TRACER, LEVELS, NX, NY), ((0, 4), (2, 8)), -0.4, 0.0), -0.2, 0.2)
    flux_y = jnp.clip(jax.random.uniform(streams_of[3], (N_TRACER, LEVELS, NX, NY), jnp.float32, -0.2, 0.2) * level_of(streams_of[3], (N_TRACER, LEVELS, NX, NY), ((0, 4), (2, 8)), -0.4, 0.0), -0.2, 0.2)
    flux_z = jnp.clip(jax.random.uniform(streams_of[4], (N_TRACER, LEVELS, NX, NY), jnp.float32, -0.05, 0.05) * level_of(streams_of[4], (N_TRACER, LEVELS, NX, NY), ((0, 4), (2, 8)), -0.4, 0.0), -0.05, 0.05)
    reactants = touch_ends(jax.random.randint(streams_of[5], (REACTIONS, 2), 0, TRACERS), jax.random.fold_in(streams_of[5], 1), 0, TRACERS - 1).astype(jnp.int32)
    products = touch_ends((jax.random.randint(streams_of[6], (REACTIONS, TRACERS), 0, TRACERS) < 3).astype(jnp.int32), jax.random.fold_in(streams_of[6], 1), 0, 1)
    rate_coeff = jnp.clip(jnp.exp(jax.random.uniform(streams_of[7], (REACTIONS,), jnp.float32, math.log(0.01), math.log(0.1))), 0.01, 0.1)
    record_of_step = jax.random.randint(streams_of[8], (STEPS,), 0, N_TRACER).astype(jnp.int32)
    return {"tracers": tracers, "air_mass": air_mass, "flux_x": flux_x, "flux_y": flux_y, "flux_z": flux_z, "reactants": reactants, "products": products, "rate_coeff": rate_coeff, "record_of_step": record_of_step}


def take_slice(values, first_cell, how_many, dim_along):
    return lax.slice_in_dim(values, first_cell, first_cell + how_many, axis=dim_along)


def pad_three(values, dim_along):
    widths = [(0, 0)] * values.ndim
    widths[dim_along] = (3, 3)
    return jnp.pad(values, widths)


def face_flux(tracer_pad, air_pad, crossing, dim_along):
    cell_count = tracer_pad.shape[dim_along] - 6
    lower = take_slice(tracer_pad, 1, cell_count + 3, dim_along)
    upper = take_slice(tracer_pad, 2, cell_count + 3, dim_along)
    outer = take_slice(tracer_pad, 0, cell_count + 3, dim_along) + take_slice(tracer_pad, 3, cell_count + 3, dim_along)
    edges = (7.0 / 12.0) * (lower + upper) - (1.0 / 12.0) * outer
    edges = jnp.clip(edges, jnp.minimum(lower, upper), jnp.maximum(lower, upper))
    left_edge = take_slice(edges, 0, cell_count + 2, dim_along)
    right_edge = take_slice(edges, 1, cell_count + 2, dim_along)
    centre = take_slice(tracer_pad, 2, cell_count + 2, dim_along)
    spread = right_edge - left_edge
    bending = 6.0 * (centre - 0.5 * (left_edge + right_edge))
    upwind_air = jnp.where(crossing > 0, take_slice(air_pad, 2, cell_count + 1, dim_along),
                           take_slice(air_pad, 3, cell_count + 1, dim_along))
    courant = jnp.abs(crossing) / jnp.maximum(upwind_air, 0.5)
    factor = 1.0 - 2.0 * courant / 3.0
    from_left = take_slice(right_edge, 0, cell_count + 1, dim_along) - 0.5 * courant * (
        take_slice(spread, 0, cell_count + 1, dim_along) - factor * take_slice(bending, 0, cell_count + 1, dim_along))
    from_right = take_slice(left_edge, 1, cell_count + 1, dim_along) + 0.5 * courant * (
        take_slice(spread, 1, cell_count + 1, dim_along) + factor * take_slice(bending, 1, cell_count + 1, dim_along))
    return crossing * jnp.where(crossing > 0, from_left, from_right)


def divergence(flux_faces, dim_along, cell_count):
    return take_slice(flux_faces, 1, cell_count, dim_along) - take_slice(flux_faces, 0, cell_count, dim_along)


def close_walls(south_flux, bottom_flux):
    row_index = lax.broadcasted_iota(jnp.int32, south_flux.shape, 3)
    level_index = lax.broadcasted_iota(jnp.int32, bottom_flux.shape, 1)
    return jnp.where(row_index == 0, 0.0, south_flux), jnp.where(level_index == 0, 0.0, bottom_flux)


def advect(tracer_xpad, air_xpad, east_faces, south_flux, bottom_flux, air_now):
    level_count = air_now.shape[1]
    row_count = air_now.shape[2]
    column_count = air_now.shape[3]
    tracer = take_slice(tracer_xpad, 3, row_count, 2)
    north_faces = jnp.concatenate([south_flux, jnp.zeros_like(take_slice(south_flux, 0, 1, 3))], 3)
    upper_faces = jnp.concatenate([bottom_flux, jnp.zeros_like(take_slice(bottom_flux, 0, 1, 1))], 1)
    flux_rows = face_flux(tracer_xpad, air_xpad, east_faces, 2)
    flux_columns = face_flux(pad_three(tracer, 3), pad_three(air_now, 3), north_faces, 3)
    flux_levels = face_flux(pad_three(tracer, 1), pad_three(air_now, 1), upper_faces, 1)
    air_next = (air_now - divergence(east_faces, 2, row_count) - divergence(north_faces, 3, column_count)
                - divergence(upper_faces, 1, level_count))
    tracer_mass = (air_now * tracer - divergence(flux_rows, 2, row_count) - divergence(flux_columns, 3, column_count)
                   - divergence(flux_levels, 1, level_count))
    return tracer_mass / air_next


def reference(tracers, air_mass, flux_x, flux_y, flux_z, reactants, products, rate_coeff, record_of_step):
    reactions, species = products.shape
    ident = lax.broadcasted_iota(jnp.int32, (reactions, species), 1)
    first_hot = (reactants[:, 0:1] == ident).astype(jnp.float32)
    second_hot = (reactants[:, 1:2] == ident).astype(jnp.float32)
    net = products.astype(jnp.float32) - first_hot - second_hot
    mixing = tracers
    for step_index in range(STEPS):
        record = record_of_step[step_index]
        air_now = lax.dynamic_index_in_dim(air_mass, record, 0, keepdims=True)
        east = lax.dynamic_index_in_dim(flux_x, record, 0, keepdims=True)
        south = lax.dynamic_index_in_dim(flux_y, record, 0, keepdims=True)
        bottom = lax.dynamic_index_in_dim(flux_z, record, 0, keepdims=True)
        row_index = lax.broadcasted_iota(jnp.int32, east.shape, 2)
        east = jnp.where(row_index == 0, 0.0, east)
        east_faces = jnp.concatenate([east, jnp.zeros_like(take_slice(east, 0, 1, 2))], 2)
        south, bottom = close_walls(south, bottom)
        air_xpad = pad_three(air_now, 2)

        def advect_one(single):
            return advect(pad_three(single[None], 2), air_xpad, east_faces, south, bottom, air_now)[0]

        advected = lax.map(advect_one, mixing)
        conc = advected.astype(jnp.bfloat16)

        def react_level(level_index):
            layer = lax.dynamic_index_in_dim(conc, level_index, 1, keepdims=False)
            flattened = layer.reshape(species, -1)
            first = jnp.take(flattened, reactants[:, 0], axis=0).astype(jnp.float32)
            second = jnp.take(flattened, reactants[:, 1], axis=0).astype(jnp.float32)
            reaction_rate = (rate_coeff[:, None] * first * second).astype(jnp.bfloat16)
            change = jnp.dot(net.T, reaction_rate.astype(jnp.float32), preferred_element_type=jnp.float32,
                             precision=lax.Precision.HIGHEST)
            return change.astype(jnp.bfloat16).reshape(layer.shape)

        increment = lax.map(react_level, jnp.arange(LEVELS, dtype=jnp.int32))
        mixing = advected + jnp.moveaxis(increment, 0, 1).astype(jnp.float32)
    return mixing
```

```python
import functools

import jax
import jax.numpy as jnp
from jax import lax
from jax.experimental import pallas as pl
from jax.experimental.pallas import tpu as pltpu
from jax.sharding import PartitionSpec as P

STEPS = 2
PIECES = 4
WIDE = 4


def face_weights(flux, mass_low, mass_high):
    courant = jnp.abs(flux) / jnp.maximum(jnp.where(flux > 0, mass_low, mass_high), 0.5)
    square = courant * courant
    return (
        flux * (1.0 - 2.0 * courant + square),
        flux * (square - courant),
        flux * (3.0 * courant - 2.0 * square),
    )


def edge_value(outer_low, low, high, outer_high):
    value = (7.0 / 12.0) * (low + high) - (1.0 / 12.0) * (outer_low + outer_high)
    return jnp.minimum(jnp.maximum(value, jnp.minimum(low, high)), jnp.maximum(low, high))


def face_value(flux, weights, edge, edge_low, edge_high, low, high):
    up = flux > 0
    return (
        weights[0] * edge
        + weights[1] * jnp.where(up, edge_low, edge_high)
        + weights[2] * jnp.where(up, low, high)
    )


def rolled_difference(q, flux, weights, axis, place):
    size = q.shape[axis]
    low = jnp.where(place >= 1, pltpu.roll(q, 1, axis), 0.0)
    outer_low = jnp.where(place >= 2, pltpu.roll(q, 2, axis), 0.0)
    outer_high = jnp.where(place < size - 1, pltpu.roll(q, size - 1, axis), 0.0)
    edge = edge_value(outer_low, low, q, outer_high)
    last = (7.0 / 12.0) * q - (1.0 / 12.0) * low
    last = jnp.minimum(jnp.maximum(last, jnp.minimum(q, 0.0)), jnp.maximum(q, 0.0))
    edge_high = jnp.where(place == size - 1, last, pltpu.roll(edge, size - 1, axis))
    faces = face_value(flux, weights, edge, pltpu.roll(edge, 1, axis), edge_high, low, q)
    return pltpu.roll(faces, size - 1, axis) - faces


def step_kernel(
    n, chunks, q_ref, low_ref, high_ref, air_ref, fx_ref, fy_ref, fz_ref, pick_ref, net_ref, rate_ref,
    out_ref, wx, wy, wz, inverse, lines, send_one, recv_one, send_two, recv_two, back,
    send_sem, recv_sem, send_sem2, recv_sem2,
):
    tracers, rows, levels, columns = q_ref.shape
    padded = back.shape[0] // (rows * levels)
    width = padded // chunks
    in_chunk = tracers // chunks
    held = rows * levels // n
    reactions = rate_ref.shape[0]
    me = lax.axis_index("tracer")
    peers = [lax.rem(me + k, n) for k in range(n)]

    barrier = pltpu.get_barrier_semaphore()
    for peer in peers[1:]:
        pl.semaphore_signal(
            barrier, inc=1, device_id={"tracer": peer}, device_id_type=pl.DeviceIdType.MESH
        )
    pl.semaphore_wait(barrier, n - 1)

    shape = (levels, columns)
    level = lax.broadcasted_iota(jnp.int32, shape, 0)
    column = lax.broadcasted_iota(jnp.int32, shape, 1)

    @pl.loop(0, rows + 1)
    def _(r):
        for i, w in enumerate(face_weights(fx_ref[r], air_ref[r], air_ref[r + 1])):
            wx[i, r] = w

    @pl.loop(0, rows)
    def _(r):
        mass = air_ref[r + 1]
        south, bottom = fy_ref[r], fz_ref[r]
        for i, w in enumerate(face_weights(south, pltpu.roll(mass, 1, 1), mass)):
            wy[i, r] = w
        for i, w in enumerate(face_weights(bottom, pltpu.roll(mass, 1, 0), mass)):
            wz[i, r] = w
        new_mass = (
            mass
            - (fx_ref[r + 1] - fx_ref[r])
            - (pltpu.roll(south, columns - 1, 1) - south)
            - (pltpu.roll(bottom, levels - 1, 0) - bottom)
        )
        inverse[r] = 1.0 / new_mass

    if in_chunk != width:
        lines[...] = jnp.zeros_like(lines)

    def copy_one(k, c):
        return pltpu.make_async_remote_copy(
            src_ref=send_one.at[peers[k], c],
            dst_ref=recv_one.at[me, c],
            send_sem=send_sem.at[k - 1, c],
            recv_sem=recv_sem.at[k - 1, c],
            device_id={"tracer": peers[k]},
            device_id_type=pl.DeviceIdType.MESH,
        )

    def arrived_one(k, c):
        source = peers[n - k]
        return pltpu.make_async_remote_copy(
            src_ref=send_one.at[source, c],
            dst_ref=recv_one.at[source, c],
            send_sem=send_sem.at[k - 1, c],
            recv_sem=recv_sem.at[k - 1, c],
            device_id={"tracer": source},
            device_id_type=pl.DeviceIdType.MESH,
        )

    for c in range(chunks):

        @pl.loop(0, in_chunk)
        def _(s):
            t = c * in_chunk + s

            def cell(r):
                if r < 0:
                    return low_ref[t, r + 3]
                return q_ref[t, r] if r < rows else high_ref[t, r - rows]

            q = {r: cell(r) for r in range(-3, 2)}
            edges = {r: edge_value(q[r - 2], q[r - 1], q[r], q[r + 1]) for r in (-1, 0)}
            before = None
            for r in range(rows + 1):
                q[r + 2] = cell(r + 2)
                edges[r + 1] = edge_value(q[r - 1], q[r], q[r + 1], q[r + 2])
                face = face_value(
                    fx_ref[r], [wx[i, r] for i in range(3)],
                    edges[r], edges[r - 1], edges[r + 1], q[r - 1], q[r],
                )
                if r > 0:
                    p = r - 1
                    total = face - before
                    total += rolled_difference(q[p], fy_ref[p], [wy[i, p] for i in range(3)], 1, column)
                    total += rolled_difference(q[p], fz_ref[p], [wz[i, p] for i in range(3)], 0, level)
                    advected = (air_ref[p + 1] * q[p] - total) * inverse[p]
                    out_ref[t, p] = advected
                    lines[pl.ds(p * levels * width + s, levels, stride=width), :] = advected
                before = face

        for d in range(n):
            size = held * width
            send_one[d, c] = (
                lines[d * size : (d + 1) * size, :].astype(jnp.bfloat16).reshape(held, width, columns)
            )
        for k in range(1, n):
            copy_one(k, c).start()
        recv_one[me, c] = send_one[me, c]

    for c in range(chunks):
        for k in range(1, n):
            arrived_one(k, c).wait_recv()

    part = held // PIECES

    def copy_two(k, h):
        span = pl.ds(h * part, part)
        return pltpu.make_async_remote_copy(
            src_ref=send_two.at[peers[k], span],
            dst_ref=recv_two.at[me, span],
            send_sem=send_sem2.at[k - 1, h],
            recv_sem=recv_sem2.at[k - 1, h],
            device_id={"tracer": peers[k]},
            device_id_type=pl.DeviceIdType.MESH,
        )

    def arrived_two(k, h):
        span = pl.ds(h * part, part)
        source = peers[n - k]
        return pltpu.make_async_remote_copy(
            src_ref=send_two.at[source, span],
            dst_ref=recv_two.at[source, span],
            send_sem=send_sem2.at[k - 1, h],
            recv_sem=recv_sem2.at[k - 1, h],
            device_id={"tracer": source},
            device_id_type=pl.DeviceIdType.MESH,
        )

    wide = min(WIDE, part)
    for h in range(PIECES):

        @pl.loop(0, part // wide)
        def _(g):
            first = h * part + g * wide
            conc = jnp.concatenate(
                [
                    jnp.concatenate(
                        [recv_one[d, c, first + i] for d in range(n) for c in range(chunks)], 0
                    )
                    for i in range(wide)
                ],
                1,
            )
            one = jnp.dot(pick_ref[:reactions], conc, preferred_element_type=jnp.float32)
            two = jnp.dot(pick_ref[reactions:], conc, preferred_element_type=jnp.float32)
            rate = (rate_ref[...] * one * two).astype(jnp.bfloat16)
            change = jnp.dot(net_ref[...], rate, preferred_element_type=jnp.float32).astype(jnp.bfloat16)
            for d in range(n):
                for i in range(wide):
                    send_two[d, first + i] = change[
                        d * padded : (d + 1) * padded, i * columns : (i + 1) * columns
                    ]

        for k in range(1, n):
            copy_two(k, h).start()
        span = pl.ds(h * part, part)
        recv_two[me, span] = send_two[me, span]

    for h in range(PIECES):
        for k in range(1, n):
            arrived_two(k, h).wait_recv()

    size = held * padded
    for d in range(n):
        back[d * size : (d + 1) * size, :] = (
            recv_two[d].astype(jnp.float32).reshape(size, columns)
        )

    @pl.loop(0, tracers)
    def _(t):
        for r in range(rows):
            out_ref[t, r] += back[pl.ds(r * levels * padded + t, levels, stride=padded), :]

    for k in range(1, n):
        for c in range(chunks):
            copy_one(k, c).wait_send()
        for h in range(PIECES):
            copy_two(k, h).wait_send()


def step(n, q, low, high, air, fx, fy, fz, pick, net, rate):
    tracers, rows, levels, columns = q.shape
    padded = net.shape[0] // n
    chunks = tracers // 16 if tracers % 16 == 0 else 1
    width = padded // chunks
    held = rows * levels // n
    vmem = pl.BlockSpec(memory_space=pltpu.VMEM)
    f32, bf16 = jnp.float32, jnp.bfloat16
    return pl.pallas_call(
        functools.partial(step_kernel, n, chunks),
        out_shape=jax.ShapeDtypeStruct(q.shape, f32),
        in_specs=[vmem] * 10,
        out_specs=vmem,
        scratch_shapes=[
            pltpu.VMEM((3, rows + 1, levels, columns), f32),
            pltpu.VMEM((3, rows, levels, columns), f32),
            pltpu.VMEM((3, rows, levels, columns), f32),
            pltpu.VMEM((rows, levels, columns), f32),
            pltpu.VMEM((rows * levels * width, columns), f32),
            pltpu.VMEM((n, chunks, held, width, columns), bf16),
            pltpu.VMEM((n, chunks, held, width, columns), bf16),
            pltpu.VMEM((n, held, padded, columns), bf16),
            pltpu.VMEM((n, held, padded, columns), bf16),
            pltpu.VMEM((rows * levels * padded, columns), f32),
            pltpu.SemaphoreType.DMA((n - 1, chunks)),
            pltpu.SemaphoreType.DMA((n - 1, chunks)),
            pltpu.SemaphoreType.DMA((n - 1, PIECES)),
            pltpu.SemaphoreType.DMA((n - 1, PIECES)),
        ],
        compiler_params=pltpu.CompilerParams(
            collective_id=0, has_side_effects=True, vmem_limit_bytes=50 * 1024 * 1024
        ),
    )(q, low, high, air, fx, fy, fz, pick, net, rate)


def halos(block, dim):
    count = lax.axis_size("tile")
    forward = [(i, i + 1) for i in range(count - 1)]
    backward = [(target, source) for source, target in forward]
    size = block.shape[dim]
    low = lax.ppermute(lax.slice_in_dim(block, size - 3, size, axis=dim), "tile", forward)
    high = lax.ppermute(lax.slice_in_dim(block, 0, 3, axis=dim), "tile", backward)
    return low, high


def pad_blocks(matrix, n, padded):
    own = matrix.shape[1] // n
    blocks = matrix.reshape(matrix.shape[0], n, own)
    return jnp.pad(blocks, ((0, 0), (0, 0), (0, padded - own))).reshape(matrix.shape[0], n * padded)


def per_device(
    tracers, air_mass, flux_x, flux_y, flux_z, reactants, products, rate_coeff, record_of_step
):
    n = lax.axis_size("tracer")
    reactions, species = products.shape
    padded = -(-tracers.shape[0] // 16) * 16
    ident = lax.broadcasted_iota(jnp.int32, (reactions, species), 1)
    first_hot = (reactants[:, 0:1] == ident).astype(jnp.float32)
    second_hot = (reactants[:, 1:2] == ident).astype(jnp.float32)
    pick = pad_blocks(jnp.concatenate([first_hot, second_hot], 0), n, padded).astype(jnp.bfloat16)
    net = pad_blocks(products.astype(jnp.float32) - first_hot - second_hot, n, padded)
    net = net.T.astype(jnp.bfloat16)
    rate = rate_coeff[:, None]
    mixing = jnp.swapaxes(tracers, 1, 2)
    rows = mixing.shape[1]
    fields = jnp.swapaxes(jnp.concatenate([air_mass, flux_x, flux_y, flux_z], 0), 1, 2)
    mine = lax.axis_index("tracer")
    chosen = jnp.stack([jnp.where(record_of_step[s] == mine, fields, 0.0) for s in range(STEPS)])
    weather = lax.psum(chosen, "tracer")
    below, above = halos(weather[:, :2], 2)
    place = lax.axis_index("tile") * rows + lax.broadcasted_iota(jnp.int32, weather.shape[2:], 0)
    level = lax.broadcasted_iota(jnp.int32, weather.shape[2:], 1)
    column = lax.broadcasted_iota(jnp.int32, weather.shape[2:], 2)
    for s in range(STEPS):
        air, east, south, bottom = (weather[s, i] for i in range(4))
        air = jnp.concatenate([below[s, 0, 2:3], air, above[s, 0, :1]], 0)
        east = jnp.concatenate([jnp.where(place == 0, 0.0, east), above[s, 1, :1]], 0)
        south = jnp.where(column == 0, 0.0, south)
        bottom = jnp.where(level == 0, 0.0, bottom)
        low, high = halos(mixing, 1)
        mixing = step(n, mixing, low, high, air, east, south, bottom, pick, net, rate)
    return jnp.swapaxes(mixing, 1, 2)


def solution(mesh):
    split = P("tracer", None, "tile", None)
    return jax.shard_map(
        per_device, mesh=mesh, in_specs=(split,) * 5 + (P(),) * 4, out_specs=split, check_vma=False
    )
```

```python
import functools

import jax
import jax.numpy as jnp
from jax import lax
from jax.experimental import pallas as pl
from jax.experimental.pallas import tpu as pltpu
from jax.sharding import PartitionSpec as P

STEPS = 2
PIECES = 4
WIDE = 4


def face_weights(flux, mass_low, mass_high):
    courant = jnp.abs(flux) / jnp.maximum(jnp.where(flux > 0, mass_low, mass_high), 0.5)
    square = courant * courant
    return (
        flux * (1.0 - 2.0 * courant + square),
        flux * (square - courant),
        flux * (3.0 * courant - 2.0 * square),
    )


def edge_value(outer_low, low, high, outer_high):
    value = (7.0 / 12.0) * (low + high) - (1.0 / 12.0) * (outer_low + outer_high)
    return jnp.minimum(jnp.maximum(value, jnp.minimum(low, high)), jnp.maximum(low, high))


def face_value(flux, weights, edge, edge_low, edge_high, low, high):
    up = flux > 0
    return (
        weights[0] * edge
        + weights[1] * jnp.where(up, edge_low, edge_high)
        + weights[2] * jnp.where(up, low, high)
    )


def rolled_difference(q, flux, weights, axis, place):
    size = q.shape[axis]
    low = jnp.where(place >= 1, pltpu.roll(q, 1, axis), 0.0)
    outer_low = jnp.where(place >= 2, pltpu.roll(q, 2, axis), 0.0)
    outer_high = jnp.where(place < size - 1, pltpu.roll(q, size - 1, axis), 0.0)
    edge = edge_value(outer_low, low, q, outer_high)
    last = (7.0 / 12.0) * q - (1.0 / 12.0) * low
    last = jnp.minimum(jnp.maximum(last, jnp.minimum(q, 0.0)), jnp.maximum(q, 0.0))
    edge_high = jnp.where(place == size - 1, last, pltpu.roll(edge, size - 1, axis))
    faces = face_value(flux, weights, edge, pltpu.roll(edge, 1, axis), edge_high, low, q)
    return pltpu.roll(faces, size - 1, axis) - faces


def greet(peers, tile, tiles):
    barrier = pltpu.get_barrier_semaphore()
    for peer in peers[1:]:
        pl.semaphore_signal(
            barrier, inc=1, device_id={"tracer": peer}, device_id_type=pl.DeviceIdType.MESH
        )
    for side in range(2):

        @pl.when(tile > 0 if side else tile < tiles - 1)
        def _(side=side):
            pl.semaphore_signal(
                barrier,
                inc=1,
                device_id={"tile": tile - 1 if side else tile + 1},
                device_id_type=pl.DeviceIdType.MESH,
            )

    sides = (tile > 0).astype(jnp.int32) + (tile < tiles - 1).astype(jnp.int32)
    pl.semaphore_wait(barrier, len(peers) - 1 + sides)


def weather_kernel(n, fields_ref, out_ref, side_send, side_recv, send_sem, recv_sem):
    kinds, rows, levels, columns = fields_ref.shape
    me = lax.axis_index("tracer")
    peers = [lax.rem(me + k, n) for k in range(n)]
    tile, tiles = lax.axis_index("tile"), lax.axis_size("tile")
    greet(peers, tile, tiles)

    def side_copy(side):
        return pltpu.make_async_remote_copy(
            src_ref=fields_ref.at[pl.ds(0, 2), 0 if side else rows - 1],
            dst_ref=out_ref.at[me, pl.ds(0, 2), rows + 1 if side else 0],
            send_sem=side_send.at[side],
            recv_sem=side_recv.at[side],
            device_id={"tile": tile - 1 if side else tile + 1},
            device_id_type=pl.DeviceIdType.MESH,
        )

    for side in range(2):

        @pl.when(tile > 0 if side else tile < tiles - 1)
        def _(side=side):
            side_copy(side).start()

    blank = jnp.zeros((levels, columns), jnp.float32)
    for kind in range(kinds):

        @pl.loop(0, rows)
        def _(r, kind=kind):
            out_ref[me, kind, r + 1] = fields_ref[kind, r]

    for kind in range(2, kinds):
        out_ref[me, kind, 0] = blank
        out_ref[me, kind, rows + 1] = blank
    for side in range(2):

        @pl.when(tile == tiles - 1 if side else tile == 0)
        def _(side=side):
            for kind in range(2):
                out_ref[me, kind, rows + 1 if side else 0] = blank

        @pl.when(tile < tiles - 1 if side else tile > 0)
        def _(side=side):
            side_copy(side).wait_recv()

    def copy(k, source, target):
        return pltpu.make_async_remote_copy(
            src_ref=out_ref.at[source],
            dst_ref=out_ref.at[source],
            send_sem=send_sem.at[k - 1],
            recv_sem=recv_sem.at[k - 1],
            device_id={"tracer": target},
            device_id_type=pl.DeviceIdType.MESH,
        )

    for k in range(1, n):
        copy(k, me, peers[k]).start()
    for k in range(1, n):
        copy(k, peers[n - k], peers[n - k]).wait_recv()
    for k in range(1, n):
        copy(k, me, peers[k]).wait_send()
    for side in range(2):

        @pl.when(tile > 0 if side else tile < tiles - 1)
        def _(side=side):
            side_copy(side).wait_send()


def all_weather(n, fields):
    kinds, rows, levels, columns = fields.shape
    vmem = pl.BlockSpec(memory_space=pltpu.VMEM)
    return pl.pallas_call(
        functools.partial(weather_kernel, n),
        out_shape=jax.ShapeDtypeStruct((n, kinds, rows + 2, levels, columns), jnp.float32),
        in_specs=[vmem],
        out_specs=vmem,
        scratch_shapes=[
            pltpu.SemaphoreType.DMA((2,)),
            pltpu.SemaphoreType.DMA((2,)),
            pltpu.SemaphoreType.DMA((n - 1,)),
            pltpu.SemaphoreType.DMA((n - 1,)),
        ],
        compiler_params=pltpu.CompilerParams(
            collective_id=1, has_side_effects=True, vmem_limit_bytes=50 * 1024 * 1024
        ),
    )(fields)


def step_kernel(
    n, chunks, q_ref, air_ref, fx_ref, fy_ref, fz_ref, pick_ref, net_ref, rate_ref,
    out_ref, wx, wy, wz, inverse, lines, send_one, recv_one, send_two, recv_two, back,
    low_ref, high_ref, send_sem, recv_sem, send_sem2, recv_sem2, side_send, side_recv,
):
    tracers, rows, levels, columns = q_ref.shape
    padded = back.shape[0] // (rows * levels)
    width = padded // chunks
    in_chunk = tracers // chunks
    held = rows * levels // n
    reactions = rate_ref.shape[0]
    me = lax.axis_index("tracer")
    peers = [lax.rem(me + k, n) for k in range(n)]

    tile, tiles = lax.axis_index("tile"), lax.axis_size("tile")
    greet(peers, tile, tiles)

    def side_copy(side, c):
        span = pl.ds(c * in_chunk, in_chunk)
        return pltpu.make_async_remote_copy(
            src_ref=q_ref.at[span, pl.ds(0 if side else rows - 3, 3)],
            dst_ref=(high_ref if side else low_ref).at[span],
            send_sem=side_send.at[side, c],
            recv_sem=side_recv.at[side, c],
            device_id={"tile": tile - 1 if side else tile + 1},
            device_id_type=pl.DeviceIdType.MESH,
        )

    for c in range(chunks):
        for side in range(2):

            @pl.when(tile > 0 if side else tile < tiles - 1)
            def _(side=side, c=c):
                side_copy(side, c).start()

    @pl.when(tile == 0)
    def _():
        low_ref[...] = jnp.zeros_like(low_ref)

    @pl.when(tile == tiles - 1)
    def _():
        high_ref[...] = jnp.zeros_like(high_ref)

    shape = (levels, columns)
    level = lax.broadcasted_iota(jnp.int32, shape, 0)
    column = lax.broadcasted_iota(jnp.int32, shape, 1)

    @pl.loop(0, rows + 1)
    def _(r):
        for i, w in enumerate(face_weights(fx_ref[r], air_ref[r], air_ref[r + 1])):
            wx[i, r] = w

    @pl.loop(0, rows)
    def _(r):
        mass = air_ref[r + 1]
        south, bottom = fy_ref[r], fz_ref[r]
        for i, w in enumerate(face_weights(south, pltpu.roll(mass, 1, 1), mass)):
            wy[i, r] = w
        for i, w in enumerate(face_weights(bottom, pltpu.roll(mass, 1, 0), mass)):
            wz[i, r] = w
        new_mass = (
            mass
            - (fx_ref[r + 1] - fx_ref[r])
            - (pltpu.roll(south, columns - 1, 1) - south)
            - (pltpu.roll(bottom, levels - 1, 0) - bottom)
        )
        inverse[r] = 1.0 / new_mass

    if in_chunk != width:
        lines[...] = jnp.zeros_like(lines)

    def copy_one(k, c):
        return pltpu.make_async_remote_copy(
            src_ref=send_one.at[peers[k], c],
            dst_ref=recv_one.at[me, c],
            send_sem=send_sem.at[k - 1, c],
            recv_sem=recv_sem.at[k - 1, c],
            device_id={"tracer": peers[k]},
            device_id_type=pl.DeviceIdType.MESH,
        )

    def arrived_one(k, c):
        source = peers[n - k]
        return pltpu.make_async_remote_copy(
            src_ref=send_one.at[source, c],
            dst_ref=recv_one.at[source, c],
            send_sem=send_sem.at[k - 1, c],
            recv_sem=recv_sem.at[k - 1, c],
            device_id={"tracer": source},
            device_id_type=pl.DeviceIdType.MESH,
        )

    for c in range(chunks):
        for side in range(2):

            @pl.when(tile < tiles - 1 if side else tile > 0)
            def _(side=side, c=c):
                side_copy(side, c).wait_recv()

        @pl.loop(0, in_chunk)
        def _(s, c=c):
            t = c * in_chunk + s

            def cell(r):
                if r < 0:
                    return low_ref[t, r + 3]
                return q_ref[t, r] if r < rows else high_ref[t, r - rows]

            q = {r: cell(r) for r in range(-3, 2)}
            edges = {r: edge_value(q[r - 2], q[r - 1], q[r], q[r + 1]) for r in (-1, 0)}
            before = None
            for r in range(rows + 1):
                q[r + 2] = cell(r + 2)
                edges[r + 1] = edge_value(q[r - 1], q[r], q[r + 1], q[r + 2])
                face = face_value(
                    fx_ref[r], [wx[i, r] for i in range(3)],
                    edges[r], edges[r - 1], edges[r + 1], q[r - 1], q[r],
                )
                if r > 0:
                    p = r - 1
                    total = face - before
                    total += rolled_difference(q[p], fy_ref[p], [wy[i, p] for i in range(3)], 1, column)
                    total += rolled_difference(q[p], fz_ref[p], [wz[i, p] for i in range(3)], 0, level)
                    advected = (air_ref[p + 1] * q[p] - total) * inverse[p]
                    out_ref[t, p] = advected
                    lines[pl.ds(p * levels * width + s, levels, stride=width), :] = advected
                before = face

        for d in range(n):
            size = held * width
            send_one[d, c] = (
                lines[d * size : (d + 1) * size, :].astype(jnp.bfloat16).reshape(held, width, columns)
            )
        for k in range(1, n):
            copy_one(k, c).start()
        recv_one[me, c] = send_one[me, c]

    for c in range(chunks):
        for k in range(1, n):
            arrived_one(k, c).wait_recv()

    part = held // PIECES

    def copy_two(k, h):
        span = pl.ds(h * part, part)
        return pltpu.make_async_remote_copy(
            src_ref=send_two.at[peers[k], span],
            dst_ref=recv_two.at[me, span],
            send_sem=send_sem2.at[k - 1, h],
            recv_sem=recv_sem2.at[k - 1, h],
            device_id={"tracer": peers[k]},
            device_id_type=pl.DeviceIdType.MESH,
        )

    def arrived_two(k, h):
        span = pl.ds(h * part, part)
        source = peers[n - k]
        return pltpu.make_async_remote_copy(
            src_ref=send_two.at[source, span],
            dst_ref=recv_two.at[source, span],
            send_sem=send_sem2.at[k - 1, h],
            recv_sem=recv_sem2.at[k - 1, h],
            device_id={"tracer": source},
            device_id_type=pl.DeviceIdType.MESH,
        )

    wide = min(WIDE, part)
    for h in range(PIECES):

        @pl.loop(0, part // wide)
        def _(g):
            first = h * part + g * wide
            conc = jnp.concatenate(
                [
                    jnp.concatenate(
                        [recv_one[d, c, first + i] for d in range(n) for c in range(chunks)], 0
                    )
                    for i in range(wide)
                ],
                1,
            )
            one = jnp.dot(pick_ref[:reactions], conc, preferred_element_type=jnp.float32)
            two = jnp.dot(pick_ref[reactions:], conc, preferred_element_type=jnp.float32)
            rate = (rate_ref[...] * one * two).astype(jnp.bfloat16)
            change = jnp.dot(net_ref[...], rate, preferred_element_type=jnp.float32).astype(jnp.bfloat16)
            for d in range(n):
                for i in range(wide):
                    send_two[d, first + i] = change[
                        d * padded : (d + 1) * padded, i * columns : (i + 1) * columns
                    ]

        for k in range(1, n):
            copy_two(k, h).start()
        span = pl.ds(h * part, part)
        recv_two[me, span] = send_two[me, span]

    for h in range(PIECES):
        for k in range(1, n):
            arrived_two(k, h).wait_recv()

    size = held * padded
    for d in range(n):
        back[d * size : (d + 1) * size, :] = (
            recv_two[d].astype(jnp.float32).reshape(size, columns)
        )

    @pl.loop(0, tracers)
    def _(t):
        for r in range(rows):
            out_ref[t, r] += back[pl.ds(r * levels * padded + t, levels, stride=padded), :]

    for c in range(chunks):
        for side in range(2):

            @pl.when(tile > 0 if side else tile < tiles - 1)
            def _(side=side, c=c):
                side_copy(side, c).wait_send()

    for k in range(1, n):
        for c in range(chunks):
            copy_one(k, c).wait_send()
        for h in range(PIECES):
            copy_two(k, h).wait_send()


def step(n, q, air, fx, fy, fz, pick, net, rate):
    tracers, rows, levels, columns = q.shape
    padded = net.shape[0] // n
    chunks = tracers // 16 if tracers % 16 == 0 else 1
    width = padded // chunks
    held = rows * levels // n
    vmem = pl.BlockSpec(memory_space=pltpu.VMEM)
    f32, bf16 = jnp.float32, jnp.bfloat16
    return pl.pallas_call(
        functools.partial(step_kernel, n, chunks),
        out_shape=jax.ShapeDtypeStruct(q.shape, f32),
        in_specs=[vmem] * 8,
        out_specs=vmem,
        scratch_shapes=[
            pltpu.VMEM((3, rows + 1, levels, columns), f32),
            pltpu.VMEM((3, rows, levels, columns), f32),
            pltpu.VMEM((3, rows, levels, columns), f32),
            pltpu.VMEM((rows, levels, columns), f32),
            pltpu.VMEM((rows * levels * width, columns), f32),
            pltpu.VMEM((n, chunks, held, width, columns), bf16),
            pltpu.VMEM((n, chunks, held, width, columns), bf16),
            pltpu.VMEM((n, held, padded, columns), bf16),
            pltpu.VMEM((n, held, padded, columns), bf16),
            pltpu.VMEM((rows * levels * padded, columns), f32),
            pltpu.VMEM((tracers, 3, levels, columns), f32),
            pltpu.VMEM((tracers, 3, levels, columns), f32),
            pltpu.SemaphoreType.DMA((n - 1, chunks)),
            pltpu.SemaphoreType.DMA((n - 1, chunks)),
            pltpu.SemaphoreType.DMA((n - 1, PIECES)),
            pltpu.SemaphoreType.DMA((n - 1, PIECES)),
            pltpu.SemaphoreType.DMA((2, chunks)),
            pltpu.SemaphoreType.DMA((2, chunks)),
        ],
        compiler_params=pltpu.CompilerParams(
            collective_id=0, has_side_effects=True, vmem_limit_bytes=50 * 1024 * 1024
        ),
    )(q, air, fx, fy, fz, pick, net, rate)


def pad_blocks(matrix, n, padded):
    own = matrix.shape[1] // n
    blocks = matrix.reshape(matrix.shape[0], n, own)
    return jnp.pad(blocks, ((0, 0), (0, 0), (0, padded - own))).reshape(matrix.shape[0], n * padded)


def per_device(
    tracers, air_mass, flux_x, flux_y, flux_z, reactants, products, rate_coeff, record_of_step
):
    n = lax.axis_size("tracer")
    reactions, species = products.shape
    padded = -(-tracers.shape[0] // 16) * 16
    ident = lax.broadcasted_iota(jnp.int32, (reactions, species), 1)
    first_hot = (reactants[:, 0:1] == ident).astype(jnp.float32)
    second_hot = (reactants[:, 1:2] == ident).astype(jnp.float32)
    pick = pad_blocks(jnp.concatenate([first_hot, second_hot], 0), n, padded).astype(jnp.bfloat16)
    net = pad_blocks(products.astype(jnp.float32) - first_hot - second_hot, n, padded)
    net = net.T.astype(jnp.bfloat16)
    rate = rate_coeff[:, None]
    mixing = jnp.swapaxes(tracers, 1, 2)
    rows = mixing.shape[1]
    fields = jnp.swapaxes(jnp.concatenate([air_mass, flux_x, flux_y, flux_z], 0), 1, 2)
    gathered = all_weather(n, fields)
    place = lax.axis_index("tile") * rows + lax.broadcasted_iota(jnp.int32, (rows + 1, 1, 1), 0)
    level = lax.broadcasted_iota(jnp.int32, fields.shape[1:], 1)
    column = lax.broadcasted_iota(jnp.int32, fields.shape[1:], 2)
    for s in range(STEPS):
        weather = lax.dynamic_index_in_dim(gathered, record_of_step[s], 0, keepdims=False)
        air = weather[0]
        east = jnp.where(place == 0, 0.0, weather[1, 1:])
        south = jnp.where(column == 0, 0.0, weather[2, 1 : rows + 1])
        bottom = jnp.where(level == 0, 0.0, weather[3, 1 : rows + 1])
        mixing = step(n, mixing, air, east, south, bottom, pick, net, rate)
    return jnp.swapaxes(mixing, 1, 2)


def solution(mesh):
    split = P("tracer", None, "tile", None)
    return jax.shard_map(
        per_device, mesh=mesh, in_specs=(split,) * 5 + (P(),) * 4, out_specs=split, check_vma=False
    )
```
